128 devices in a mesh: row: 8 (over z_hi, x), col: 16 (over y, z_lo, core).
Axes of the slice: x: 4, y: 4, z: 4 (z_hi: 2, z_lo: 2; z = z_hi * 2 + z_lo), core: 2. Of those that a mesh axis runs over, the one named last changes fastest.
Arguments:
- pair_repr: bfloat16 [1024, 1024, 128], P('row', 'col'), may hold values from -6 to 6
- logit_cotangent: bfloat16 [1024, 1024, 128], P('row', 'col'), may hold values from -6 to 6
- pair_mask: int32 [1024, 1024], P('row', 'col'), may hold values 0 or 1
- single_repr: bfloat16 [1024, 384], P(('row', 'col')), may hold values from -6 to 6
- token_index: int32 [1024], replicated, may hold values from 0 to 2046, as said below
- pair_up: bfloat16 [128, 512], replicated, may hold values from -0.5 to 0.5
- pair_gate: bfloat16 [128, 512], replicated, may hold values from -0.5 to 0.5
- pair_down: bfloat16 [512, 128], replicated, may hold values from -0.25 to 0.25
- head_weight: bfloat16 [128, 128], replicated, may hold values from -0.5 to 0.5
- rel_table: bfloat16 [65, 128], replicated, may hold values from -3 to 3
- proj_row: bfloat16 [384, 128], replicated, may hold values from -0.3125 to 0.3125
- proj_col: bfloat16 [384, 128], replicated, may hold values from -0.3125 to 0.3125
- single_gate: bfloat16 [384, 1536], replicated, may hold values from -0.3125 to 0.3125
- single_up: bfloat16 [384, 1536], replicated, may hold values from -0.3125 to 0.3125
- single_down: bfloat16 [1536, 384], replicated, may hold values from -0.15625 to 0.15625
Outputs:
- pair_grad: bfloat16 [1024, 1024, 128], P('row', 'col')
- single_grad: bfloat16 [1024, 384], P(('row', 'col'))
- grad_pair_up: float32 [128, 512], replicated
- grad_pair_gate: float32 [128, 512], replicated
- grad_pair_down: float32 [512, 128], replicated
- grad_head: float32 [128, 128], replicated
- grad_rel: float32 [65, 128], replicated
- grad_proj_row: float32 [384, 128], replicated
- grad_proj_col: float32 [384, 128], replicated
- grad_single_gate: float32 [384, 1536], P(None, ('row', 'col'))
- grad_single_up: float32 [384, 1536], P(None, ('row', 'col'))
- grad_single_down: float32 [1536, 384], P(('row', 'col'))
The draws below stay inside these ranges and needn't reach their ends.
Inputs may be any that keep to these rules, and one draw needn't show every extreme that they name: `token_index`: strictly increasing, entry 0 is 0, successive entries differ by 1 to 3, the last entry is 2046.
All inputs are finite; a program needn't handle non-finite values. No bound on the sum of `pair_mask` on one device may be relied on, other than what follows from the above.
Results may differ from the reference program's by a relative error of at most 0.018.
Values may be sent and summed in bfloat16 or wider, within the bound.
A program may use at most 128 MiB of HBM per device.

```python
import jax
import jax.numpy as jnp
from jax import lax

CZ = 128
HID = 512
NB = 64
CS = 384
SH = 1536
NREL = 65
TOKENS = 1024


def draw_token_index(key, part):
    places = jnp.arange(TOKENS, dtype=jnp.int32)
    shifts = jax.random.randint(key, (TOKENS,), -1, 1)
    ends = (places == 0) | (places == TOKENS - 1)
    shifts = jnp.where(ends, 0, shifts)
    return (2 * places + shifts).astype(jnp.int32)


def touch_ends(entries, own_key, low, largest):
    index_at = [jax.random.randint(jax.random.fold_in(own_key, axis), (), 0, length) for axis, length in enumerate(entries.shape)]
    main_axis = entries.shape.index(max(entries.shape))
    beside = index_at[:main_axis] + [(index_at[main_axis] + 1) % entries.shape[main_axis]] + index_at[main_axis + 1:]
    return entries.at[tuple(index_at)].set(low).at[tuple(beside)].set(largest)


def levels(stream_key, shape, shards, least, largest):
    def one(dim, parts):
        draws = jax.random.uniform(jax.random.fold_in(jax.random.fold_in(stream_key, 6), dim), (parts,), jnp.float32, least / len(shards), largest / len(shards))
        return jnp.repeat(jnp.exp(draws), shape[dim] // parts).reshape((-1,) + (1,) * (len(shape) - dim - 1))

    loudness = one(*shards[0])
    for cut in shards[1:]:
        loudness = loudness * one(*cut)
    return loudness


def noise(stream_key, shape, scale, limit, cuts=(), held_as=jnp.bfloat16):
    gain = levels(stream_key, shape, cuts, -0.22, 0.18) if cuts else 1.0
    array = jax.random.normal(stream_key, shape, jnp.float32) * scale * gain
    return jnp.minimum(jnp.maximum(array, -limit), limit).astype(held_as)


def setup_inputs(seed: int = 0) -> dict:
    keys = jax.random.split(jax.random.key(seed), 16)
    pair_repr = noise(keys[0], (TOKENS, TOKENS, CZ), 1.0, 6.0, ((0, 8), (1, 16)))
    logit_cotangent = noise(keys[1], (TOKENS, TOKENS, 2 * NB), 1.0, 6.0, ((0, 8), (1, 16)))
    pair_mask = touch_ends((jax.random.randint(keys[2], (TOKENS, TOKENS), 0, 8) < 7).astype(jnp.int32), jax.random.fold_in(keys[2], 1), 0, 1)
    single_repr = noise(keys[3], (TOKENS, CS), 1.0, 6.0, ((0, 128),))
    token_index = draw_token_index(jax.random.fold_in(keys[15], 71), 0)
    pair_up = noise(keys[5], (CZ, HID), CZ ** -0.5, 0.5)
    pair_gate = noise(keys[6], (CZ, HID), CZ ** -0.5, 0.5)
    pair_down = noise(keys[7], (HID, CZ), HID ** -0.5, 0.25)
    head_weight = noise(keys[8], (CZ, 2 * NB), CZ ** -0.5, 0.5)
    rel_table = noise(keys[9], (NREL, CZ), 0.5, 3.0)
    proj_row = noise(keys[10], (CS, CZ), CS ** -0.5, 0.3125)
    proj_col = noise(keys[11], (CS, CZ), CS ** -0.5, 0.3125)
    single_gate = noise(keys[12], (CS, SH), CS ** -0.5, 0.3125)
    single_up = noise(keys[13], (CS, SH), CS ** -0.5, 0.3125)
    single_down = noise(keys[14], (SH, CS), SH ** -0.5, 0.15625)
    return {"pair_repr": pair_repr, "logit_cotangent": logit_cotangent, "pair_mask": pair_mask, "single_repr": single_repr, "token_index": token_index, "pair_up": pair_up, "pair_gate": pair_gate, "pair_down": pair_down, "head_weight": head_weight, "rel_table": rel_table, "proj_row": proj_row, "proj_col": proj_col, "single_gate": single_gate, "single_up": single_up, "single_down": single_down}


norm_eps = 1e-05

def gated_parts(gate):
    sigma = jax.nn.sigmoid(gate)
    return (gate * sigma, sigma * (1.0 + gate * (1.0 - sigma)))

def product(matrix_a, matrix_b):
    return jnp.dot(matrix_a, matrix_b, preferred_element_type=jnp.float32)

def product_left(matrix_a, matrix_b):
    return lax.dot_general(matrix_a, matrix_b, (((0,), (0,)), ((), ())), preferred_element_type=jnp.float32)

def product_right(matrix_a, matrix_b):
    return lax.dot_general(matrix_a, matrix_b, (((1,), (1,)), ((), ())), preferred_element_type=jnp.float32)

def single_forward(single_repr, single_gate, single_up, single_down):
    source = single_repr.astype(jnp.float32)
    inverse_rms = lax.rsqrt(lax.optimization_barrier(jnp.mean(source * source, axis=-1, keepdims=True)) + norm_eps)
    normed = source * inverse_rms
    normed_bf = normed.astype(jnp.bfloat16)
    gate_pre = product(normed_bf, single_gate)
    up_pre = product(normed_bf, single_up)
    silu_value, silu_slope = gated_parts(gate_pre)
    hidden = (silu_value * up_pre).astype(jnp.bfloat16)
    updated = (source + product(hidden, single_down)).astype(jnp.bfloat16)
    return (normed, inverse_rms, normed_bf, up_pre, silu_value, silu_slope, hidden, updated)

def single_backward(grad_in, saved_state, single_gate, single_up, single_down):
    normed, inverse_rms, normed_bf, up_pre, silu_value, silu_slope, hidden, updated = saved_state
    grad_bf = grad_in.astype(jnp.bfloat16)
    down_sum = product_left(hidden, grad_bf)
    grad_hidden = product_right(grad_bf, single_down)
    grad_up = (grad_hidden * silu_value).astype(jnp.bfloat16)
    grad_gate = (grad_hidden * up_pre * silu_slope).astype(jnp.bfloat16)
    gate_sum = product_left(normed_bf, grad_gate)
    up_sum = product_left(normed_bf, grad_up)
    grad_normed = product_right(grad_gate, single_gate) + product_right(grad_up, single_up)
    grad_source = grad_in + inverse_rms * (grad_normed - normed * lax.optimization_barrier(jnp.mean(grad_normed * normed, axis=-1, keepdims=True)))
    return (grad_source, gate_sum, up_sum, down_sum)

def pair_block(pair_blk, cot_blk, mirror_blk, row_blk, col_blk, row_pos, col_pos, rel_table, up_gate, pair_down, head_weight):
    n_rows, n_cols, pair_width = pair_blk.shape
    bin_count = mirror_blk.shape[2]
    rel_count = rel_table.shape[0]
    rel_span = (rel_count - 1) // 2
    pair_count = n_rows * n_cols
    offset = jnp.clip(row_pos[:, None] - col_pos[None, :], -rel_span, rel_span) + rel_span
    one_hot = offset.reshape(pair_count, 1) == jnp.arange(rel_count, dtype=jnp.int32)[None, :]
    hot_table = one_hot.astype(jnp.bfloat16)
    pair_in = pair_blk.astype(jnp.float32) + row_blk.astype(jnp.float32)[:, None, :] + col_blk.astype(jnp.float32)[None, :, :]
    pair_in = pair_in.reshape(pair_count, pair_width) + product(hot_table, rel_table)
    centred = pair_in - lax.optimization_barrier(jnp.mean(pair_in, axis=-1, keepdims=True))
    inv_std = lax.rsqrt(lax.optimization_barrier(jnp.mean(centred * centred, axis=-1, keepdims=True)) + norm_eps)
    normed = centred * inv_std
    normed_bf = normed.astype(jnp.bfloat16)
    hidden_width = up_gate.shape[1] // 2
    both_pre = product(normed_bf, up_gate)
    up_pre = both_pre[:, :hidden_width]
    gate_pre = both_pre[:, hidden_width:]
    silu_value, silu_slope = gated_parts(gate_pre)
    hidden = (silu_value * up_pre).astype(jnp.bfloat16)
    pair_out = (pair_in + product(hidden, pair_down)).astype(jnp.bfloat16)
    cot_flat = cot_blk.reshape(pair_count, 2 * bin_count)
    symmetric = (cot_flat[:, bin_count:].astype(jnp.float32) + mirror_blk.reshape(pair_count, bin_count).astype(jnp.float32)).astype(jnp.bfloat16)
    head_cot = jnp.concatenate([cot_flat[:, :bin_count], symmetric], axis=1)
    grad_out = product_right(head_cot, head_weight)
    grad_out_bf = grad_out.astype(jnp.bfloat16)
    grad_hidden = product_right(grad_out_bf, pair_down)
    grad_both = jnp.concatenate([(grad_hidden * silu_value).astype(jnp.bfloat16), (grad_hidden * up_pre * silu_slope).astype(jnp.bfloat16)], axis=1)
    grad_normed = product_right(grad_both, up_gate)
    grad_in = grad_out + inv_std * (grad_normed - lax.optimization_barrier(jnp.mean(grad_normed, axis=-1, keepdims=True)) - normed * lax.optimization_barrier(jnp.mean(grad_normed * normed, axis=-1, keepdims=True)))
    head_sum = product_left(pair_out, head_cot)
    down_sum = product_left(hidden, grad_out_bf)
    up_gate_sum = product_left(normed_bf, grad_both)
    rel_sum = lax.dot_general(one_hot.astype(jnp.float32), grad_in, (((0,), (0,)), ((), ())), precision=lax.Precision.HIGHEST, preferred_element_type=jnp.float32)
    grad_tile = grad_in.reshape(n_rows, n_cols, pair_width)
    return (grad_tile.astype(jnp.bfloat16), lax.optimization_barrier(jnp.sum(grad_tile, axis=1)), lax.optimization_barrier(jnp.sum(grad_tile, axis=0)), up_gate_sum, down_sum, head_sum, rel_sum)

def reference(pair_repr, logit_cotangent, pair_mask, single_repr, token_index, pair_up, pair_gate, pair_down, head_weight, rel_table, proj_row, proj_col, single_gate, single_up, single_down):
    saved_state = single_forward(single_repr, single_gate, single_up, single_down)
    updated = saved_state[7]
    row_proj = product(updated, proj_row).astype(jnp.bfloat16)
    col_proj = product(updated, proj_col).astype(jnp.bfloat16)
    masked = logit_cotangent * pair_mask[:, :, None].astype(jnp.bfloat16)
    mirrored = jnp.swapaxes(masked[:, :, NB:], 0, 1)
    up_gate = jnp.concatenate([pair_up, pair_gate], axis=1)
    block_rows = 64
    n_blocks = TOKENS // block_rows

    def block_step(running, inputs):
        pair_blk, cot_blk, mirror_blk, row_blk, pos_blk = inputs
        grad_blk, row_sum, col_sum, up_gate_sum, down_sum, head_sum, rel_sum = pair_block(pair_blk, cot_blk, mirror_blk, row_blk, col_proj, pos_blk, token_index, rel_table, up_gate, pair_down, head_weight)
        running = (running[0] + col_sum, running[1] + up_gate_sum, running[2] + down_sum, running[3] + head_sum, running[4] + rel_sum)
        return (running, (grad_blk, row_sum))
    initial = (jnp.zeros((TOKENS, CZ), jnp.float32), jnp.zeros((CZ, 2 * HID), jnp.float32), jnp.zeros((HID, CZ), jnp.float32), jnp.zeros((CZ, 2 * NB), jnp.float32), jnp.zeros((NREL, CZ), jnp.float32))
    sliced = (pair_repr.reshape(n_blocks, block_rows, TOKENS, CZ), masked.reshape(n_blocks, block_rows, TOKENS, 2 * NB), mirrored.reshape(n_blocks, block_rows, TOKENS, NB), row_proj.reshape(n_blocks, block_rows, CZ), token_index.reshape(n_blocks, block_rows))
    sums_out, blocks_out = lax.scan(block_step, initial, sliced)
    col_total, up_gate_sum, down_sum, head_sum, rel_sum = sums_out
    grad_blocks, row_sums = blocks_out
    pair_grad = grad_blocks.reshape(TOKENS, TOKENS, CZ)
    row_bf = row_sums.reshape(TOKENS, CZ).astype(jnp.bfloat16)
    col_bf = col_total.astype(jnp.bfloat16)
    single_cot = product_right(row_bf, proj_row) + product_right(col_bf, proj_col)
    prow_sum = product_left(updated, row_bf)
    pcol_sum = product_left(updated, col_bf)
    grad_source, gate_sum, up_sum, sdown_sum = single_backward(single_cot, saved_state, single_gate, single_up, single_down)
    grad_scale = 1.0 / TOKENS
    return (pair_grad, grad_source.astype(jnp.bfloat16), up_gate_sum[:, :HID] * grad_scale, up_gate_sum[:, HID:] * grad_scale, down_sum * grad_scale, head_sum * grad_scale, rel_sum * grad_scale, prow_sum * grad_scale, pcol_sum * grad_scale, gate_sum * grad_scale, up_sum * grad_scale, sdown_sum * grad_scale)
```

```python
import jax
import jax.numpy as jnp
from jax import lax
from jax.experimental import pallas as pl
from jax.experimental.pallas import tpu as pltpu
from jax.sharding import PartitionSpec as P

F = jnp.float32
B = jnp.bfloat16
MESH = pl.DeviceIdType.MESH
NR, NC = 8, 16
EPS = 1e-05
BR = 32
SHARE = 112


def mm(a, b):
    return lax.dot_general(a, b, (((1,), (0,)), ((), ())), preferred_element_type=F)


def nt(a, b):
    return lax.dot_general(a, b, (((1,), (1,)), ((), ())), preferred_element_type=F)


def tn(a, b):
    return lax.dot_general(a, b, (((0,), (0,)), ((), ())), preferred_element_type=F)


def sigmoid(v):
    return 0.5 * jnp.tanh(0.5 * v) + 0.5


def local_wait(ref, sem):
    pltpu.make_async_copy(ref, ref, sem).wait()


def kernel(
    pair_hbm, cot_hbm, mask, single, tok, tok_s, up, gate, down, head, rel, prow, pcol,
    sgate, sup, sdown,
    og, osg, oup, ogate, odown, ohead, orel, opr, opc, osgate, osup, osdown,
    pairv, cotv, ogv, lo, hi, pos, srel, smask, tbuf, sendm, mirb, sb, rowp, colp,
    arow, acol, aug, adn, ahd, arl, ws, wr, w2, w3, rr, cr, tb, cots,
    in_sem, out_sem, msend, mrecv, gsend, grecv, csend, crecv, hsend, hrecv,
    p1s, p1r, rs1, rr1, cs1, cr1, p2s, p2r, t2s, t2r, p3s, p3r, t3s, t3r,
):
    r = lax.axis_index("row")
    c = lax.axis_index("col")
    joint = r * NC + c
    diag = c // 2 == r

    cot_in = pltpu.make_async_copy(cot_hbm, cotv, in_sem.at[0])
    cot_in.start()
    pair_in = pltpu.make_async_copy(pair_hbm, pairv, in_sem.at[1])
    pair_in.start()

    bar = pltpu.get_barrier_semaphore()
    for d in range(1, NC):
        pl.semaphore_signal(bar, inc=1, device_id=(r, lax.rem(c + d, NC)), device_id_type=MESH)
    for d in range(1, NR):
        pl.semaphore_signal(bar, inc=1, device_id=(lax.rem(r + d, NR), c), device_id_type=MESH)
    for h in range(2):
        @pl.when(jnp.logical_not(jnp.logical_and(diag, c % 2 == h)))
        def _():
            pl.semaphore_signal(bar, inc=1, device_id=(c // 2, 2 * r + h), device_id_type=MESH)

    lane = lax.broadcasted_iota(jnp.int32, (64, 128), 1)
    trow = jnp.broadcast_to(tok[pl.ds(c // 2, 1), :].astype(F), (128, 128))
    pos[...] = jnp.transpose(trow)
    e = pos[pl.ds((c % 2) * 64, 64), :].astype(jnp.int32) + lane - 32
    big = jnp.int32(1 << 20)
    lo[...] = jnp.where(lane == 0, -big, jnp.where(lane > 64, big, e))
    hi[...] = jnp.where(lane == 64, big, jnp.where(lane > 64, -big, e))
    srel[...] = jnp.zeros_like(srel)
    srel[0:65, :] = rel[...].astype(F)
    mt = jnp.transpose(mask[...].astype(F))
    for b in range(4):
        smask[b] = mt[:, b * 32:(b + 1) * 32]
    for a in (acol, aug, adn, ahd, arl):
        a[...] = jnp.zeros_like(a)

    src = single[...].astype(F)
    inv_rms = lax.rsqrt(jnp.mean(src * src, axis=-1, keepdims=True) + EPS)
    normed = src * inv_rms
    nbf = normed.astype(B)
    s_gate = mm(nbf, sgate[...])
    s_up = mm(nbf, sup[...])
    s_sig = sigmoid(s_gate)
    s_silu = s_gate * s_sig
    s_hid = (s_silu * s_up).astype(B)
    updated = src + mm(s_hid, sdown[...])
    for k in range(3):
        ks = slice(k * 128, (k + 1) * 128)
        sb[r, c, k] = jnp.concatenate([src[:, ks], updated[:, ks]], axis=0).astype(B)

    pl.semaphore_wait(bar, NC + NR - jnp.where(diag, 1, 0))

    def col_copies(src_ref, dst_ref, ss, rs):
        return [
            pltpu.make_async_remote_copy(
                src_ref=src_ref(lax.rem(c + d, NC)), dst_ref=dst_ref, send_sem=ss.at[d], recv_sem=rs.at[d],
                device_id=(r, lax.rem(c + d, NC)), device_id_type=MESH,
            )
            for d in range(1, NC)
        ]

    def row_copies(src_ref, dst_ref, ss, rs):
        return [
            pltpu.make_async_remote_copy(
                src_ref=src_ref(lax.rem(r + d, NR)), dst_ref=dst_ref, send_sem=ss.at[d], recv_sem=rs.at[d],
                device_id=(lax.rem(r + d, NR), c), device_id_type=MESH,
            )
            for d in range(1, NR)
        ]

    def start(copies):
        for cp in copies:
            cp.start()

    def wait(copies):
        for cp in copies:
            cp.wait()

    strips = col_copies(lambda j: sb.at[r, c], sb.at[r, c], gsend, grecv)
    start(strips)

    cot_in.wait()
    half_lane = lax.broadcasted_iota(jnp.int32, (16, 128), 1) < 64
    for h in range(2):
        @pl.loop(0, 2)
        def _(b):
            p0 = h * 64 + b * 32
            sm = smask[2 * h + b]
            for i in range(32):
                v = cotv[p0 + i].astype(F) * jnp.broadcast_to(sm[:, i:i + 1], (64, 128))
                cotv[p0 + i] = v.astype(B)
                for t in range(2):
                    first = pltpu.roll(v[32 * t:32 * t + 16], 64, 1)
                    second = v[32 * t + 16:32 * t + 32]
                    at = pl.multiple_of((b * 32 + i) * 16, 16)
                    tbuf[t, pl.ds(at, 16), :] = jnp.where(half_lane, first, second)
        for t in range(2):
            for k in range(16):
                sendm[t, h, k] = tbuf[t, pl.ds(k, 64, stride=16), :].astype(B)
    for t in range(2):
        for h in range(2):
            own = jnp.logical_and(diag, c % 2 == h)

            @pl.when(own)
            def _():
                pltpu.make_async_copy(sendm.at[t, h], mirb.at[c % 2, t], mrecv.at[c % 2, t]).start()

            @pl.when(jnp.logical_not(own))
            def _():
                pltpu.make_async_remote_copy(
                    src_ref=sendm.at[t, h], dst_ref=mirb.at[c % 2, t], send_sem=msend.at[t, h],
                    recv_sem=mrecv.at[c % 2, t], device_id=(c // 2, 2 * r + h), device_id_type=MESH,
                ).start()

    wait(strips)
    row_u = [sb[r, :, k].astype(F)[:, 8:].reshape(128, 128).astype(B) for k in range(3)]
    rowp[...] = sum(mm(row_u[k], prow[k * 128:(k + 1) * 128]) for k in range(3)).astype(B).astype(F)

    cols = row_copies(lambda j: colp, colp, csend, crecv)

    @pl.when(diag)
    def _():
        full = sum(mm(row_u[k], pcol[k * 128:(k + 1) * 128]) for k in range(3))
        pos[...] = full
        colp[...] = pos[pl.ds((c % 2) * 64, 64), :].astype(B)
        start(cols)

    spread = row_copies(lambda j: sb.at[r], sb.at[r], hsend, hrecv)
    start(spread)

    @pl.when(jnp.logical_not(diag))
    def _():
        for d in range(1, NR):
            @pl.when(lax.rem(c // 2 + d, NR) == r)
            def _():
                local_wait(colp, crecv.at[d])

    @pl.when(diag)
    def _():
        for cp in cols:
            cp.wait_send()

    pair_in.wait()
    lane3 = lax.broadcasted_iota(jnp.int32, (1, 1, 128), 2)

    @pl.loop(0, 4)
    def _(b):
        s = b % 2
        t = b // 2
        i0 = pl.multiple_of(s * 64 + t * 32, 32)
        local_wait(mirb.at[s, t], mrecv.at[s, t])
        m = BR * 64
        hots = []
        for k in range(BR):
            at = tok_s[r * 128 + i0 + k]
            hots.append(jnp.where((lo[...] <= at) & (hi[...] >= at), F(1), F(0)).astype(B))
        hot = jnp.concatenate(hots, axis=0)
        x = (
            pairv[pl.ds(i0, BR)].astype(F)
            + rowp[pl.ds(i0, BR)][:, None, :]
            + colp[...].astype(F)[None]
        )
        x = x.reshape(m, 128) + mm(hot, srel[...].astype(B))
        cen = x - jnp.mean(x, axis=-1, keepdims=True)
        inv = lax.rsqrt(jnp.mean(cen * cen, axis=-1, keepdims=True) + EPS)
        nm = cen * inv
        nb = nm.astype(B)
        u = mm(nb, up[...])
        g = mm(nb, gate[...])
        sg = sigmoid(g)
        si = g * sg
        hid = (si * u).astype(B)
        po = (x + mm(hid, down[...])).astype(B)
        mv = mirb[s, t].astype(F)
        first = pltpu.roll(mv.reshape(1024, 128), 64, 1).reshape(16, 64, 128)
        mir = jnp.where(lane3 >= 64, jnp.concatenate([first, mv], axis=0), 0.0)
        hc = (cotv[pl.ds(i0, BR)].astype(F) + mir).astype(B).reshape(m, 128)
        go = nt(hc, head[...])
        gb = go.astype(B)
        gh = nt(gb, down[...])
        gu = (gh * si).astype(B)
        gg = (gh * u * (sg + si * (1.0 - sg))).astype(B)
        gn = nt(gu, up[...]) + nt(gg, gate[...])
        gx = go + inv * (
            gn - jnp.mean(gn, axis=-1, keepdims=True) - nm * jnp.mean(gn * nm, axis=-1, keepdims=True)
        )
        gt = gx.reshape(BR, 64, 128)
        gxb = gx.astype(B)
        ogv[pl.ds(i0, BR)] = gxb.reshape(BR, 64, 128)
        pltpu.make_async_copy(ogv.at[pl.ds(i0, BR)], og.at[pl.ds(i0, BR)], out_sem.at[b]).start()
        arow[pl.ds(i0, BR)] = jnp.sum(gt, axis=1)
        acol[...] += jnp.sum(gt, axis=0)
        aug[:, :512] += tn(nb, gu)
        aug[:, 512:] += tn(nb, gg)
        adn[...] += tn(gb, hid)
        ahd[...] += tn(po, hc)
        arl[...] += tn(hot, gxb)

    for k in range(8):
        ws[k * 128:(k + 1) * 128] = aug[:, k * 128:(k + 1) * 128].astype(B)
    for k in range(4):
        ws[1024 + k * 128:1152 + k * 128] = adn[:, k * 128:(k + 1) * 128].astype(B)
    ws[1536:1664] = ahd[...].astype(B)
    ws[1664:1792] = arl[...].astype(B)
    share = lambda j: pl.ds(pl.multiple_of(j * SHARE, 16), SHARE)
    strip = lambda j: pl.ds(pl.multiple_of(j * 8, 8), 8)
    s_row = col_copies(lambda j: arow.at[strip(j)], rr.at[c], rs1, rr1)
    s_col = row_copies(lambda j: acol.at[strip(j)], cr.at[r], cs1, cr1)
    s_w = col_copies(lambda j: ws.at[share(j)], wr.at[c], p1s, p1r)
    start(s_row)
    start(s_col)
    start(s_w)
    wr[c] = ws[share(c)]
    rr[c] = arow[strip(c)]
    cr[r] = acol[strip(r)]

    wait(spread)
    s_all = [sb[:, :, k].astype(F)[:, :, :8].reshape(1024, 128) for k in range(3)]
    u_all = jnp.concatenate(
        [sb[:, :, k].astype(F)[:, :, 8:].reshape(1024, 128).astype(B) for k in range(3)], axis=1
    )
    s_all = jnp.concatenate(s_all, axis=1)
    nb_all = (s_all * lax.rsqrt(jnp.mean(s_all * s_all, axis=-1, keepdims=True) + EPS)).astype(B)
    picks = lax.broadcasted_iota(jnp.int32, (128, 1536), 1)
    unit = lax.broadcasted_iota(jnp.int32, (128, 1536), 0)
    pick = jnp.where((picks == joint * 12 + unit) & (unit < 12), F(1), F(0)).astype(B)
    own_gate = nt(pick, sgate[...]).astype(B)
    own_up = nt(pick, sup[...]).astype(B)
    own_down = mm(pick, sdown[...]).astype(B)
    g12 = nt(nb_all, own_gate)
    u12 = nt(nb_all, own_up)
    sg12 = sigmoid(g12)
    si12 = g12 * sg12
    slope12 = u12 * (sg12 + si12 * (1.0 - sg12))
    h12 = (si12 * u12).astype(B)

    wait(s_row)
    wait(s_col)
    row_own = rr[0]
    for k in range(1, NC):
        row_own = row_own + rr[k]
    col_own = cr[0]
    for k in range(1, NR):
        col_own = col_own + cr[k]
    tb[c, r] = jnp.concatenate([row_own, col_own], axis=0).astype(B)
    t2 = row_copies(lambda j: tb.at[c, r], tb.at[c, r], t2s, t2r)
    start(t2)
    wait(s_w)
    w = wr[0].astype(F)
    for k in range(1, NC):
        w = w + wr[k].astype(F)
    w2[r] = w.astype(B)
    s2 = row_copies(lambda j: w2.at[r], w2.at[r], p2s, p2r)
    start(s2)
    wait(t2)
    t3 = col_copies(lambda j: tb.at[c], tb.at[c], t3s, t3r)
    start(t3)
    wait(s2)
    w = w2[0].astype(F)
    for k in range(1, NR):
        w = w + w2[k].astype(F)
    w3[share(c)] = w.astype(B)
    s3 = col_copies(lambda j: w3.at[share(c)], w3.at[share(c)], p3s, p3r)
    start(s3)

    scale = 1.0 / 1024
    wait(t3)
    tf = tb[...].astype(F)
    row_all = jnp.swapaxes(tf[:, :, :8], 0, 1).reshape(1024, 128).astype(B)
    col_all = tf[:, :, 8:].reshape(1024, 128).astype(B)
    cot_all = nt(row_all, prow[...]) + nt(col_all, pcol[...])
    cots[...] = cot_all
    cb = cot_all.astype(B)
    gsh = nt(cb, own_down)
    gsu = (gsh * si12).astype(B)
    gsg = (gsh * slope12).astype(B)
    osgate[...] = tn(nb_all, gsg)[:, :12] * scale
    osup[...] = tn(nb_all, gsu)[:, :12] * scale
    osdown[...] = tn(h12, cb)[:12] * scale
    opr[...] = tn(u_all, row_all) * scale
    opc[...] = tn(u_all, col_all) * scale
    c8 = cots[pl.ds(pl.multiple_of(joint * 8, 8), 8), :]
    g8 = nt(c8.astype(B), sdown[...])
    gu8 = (g8 * s_silu).astype(B)
    gg8 = (g8 * s_up * (s_sig + s_silu * (1.0 - s_sig))).astype(B)
    gn8 = nt(gg8, sgate[...]) + nt(gu8, sup[...])
    osg[...] = (
        c8 + inv_rms * (gn8 - normed * jnp.mean(gn8 * normed, axis=-1, keepdims=True))
    ).astype(B)

    wait(s3)
    for k in range(4):
        ks = slice(k * 128, (k + 1) * 128)
        oup[:, ks] = w3[k * 128:(k + 1) * 128].astype(F) * scale
        ogate[:, ks] = w3[512 + k * 128:640 + k * 128].astype(F) * scale
        odown[ks, :] = jnp.transpose(w3[1024 + k * 128:1152 + k * 128].astype(F)) * scale
    ohead[...] = w3[1536:1664].astype(F) * scale
    orel[...] = (w3[1664:1792].astype(F) * scale)[:65]

    for t in range(2):
        for h in range(2):
            @pl.when(jnp.logical_not(jnp.logical_and(diag, c % 2 == h)))
            def _():
                local_wait(sendm.at[t, h], msend.at[t, h])
    for b in range(4):
        i0 = (b % 2) * 64 + (b // 2) * 32
        pltpu.make_async_copy(ogv.at[pl.ds(i0, BR)], og.at[pl.ds(i0, BR)], out_sem.at[b]).wait()


def local(
    pair_repr, logit_cotangent, pair_mask, single_repr, token_index, pair_up, pair_gate, pair_down,
    head_weight, rel_table, proj_row, proj_col, single_gate, single_up, single_down,
):
    S = lambda shape, dtype=F: jax.ShapeDtypeStruct(shape, dtype)
    V = pl.BlockSpec(memory_space=pltpu.VMEM)
    H = pl.BlockSpec(memory_space=pl.ANY)
    vm = lambda *shape: pltpu.VMEM(shape, F)
    vb = lambda *shape: pltpu.VMEM(shape, B)
    dma = lambda *shape: pltpu.SemaphoreType.DMA(shape)
    return pl.pallas_call(
        kernel,
        out_shape=(
            S((128, 64, 128), B), S((8, 384), B), S((128, 512)), S((128, 512)), S((512, 128)),
            S((128, 128)), S((65, 128)), S((384, 128)), S((384, 128)), S((384, 12)), S((384, 12)),
            S((12, 384)),
        ),
        in_specs=[H, H, V, V, V, pl.BlockSpec(memory_space=pltpu.SMEM)] + [V] * 10,
        out_specs=[H] + [V] * 11,
        scratch_shapes=[
            vb(128, 64, 128), vb(128, 64, 128), vb(128, 64, 128),
            pltpu.VMEM((64, 128), jnp.int32), pltpu.VMEM((64, 128), jnp.int32), vm(128, 128), vm(128, 128),
            vm(4, 64, 32), vm(2, 1024, 128), vb(2, 2, 16, 64, 128), vb(2, 2, 16, 64, 128),
            vb(8, 16, 3, 16, 128), vm(128, 128), vb(64, 128),
            vm(128, 128), vm(64, 128), vm(128, 1024), vm(128, 512), vm(128, 128), vm(128, 128),
            vb(1792, 128), vb(16, SHARE, 128), vb(8, SHARE, 128), vb(1792, 128),
            vm(16, 8, 128), vm(8, 8, 128), vb(16, 8, 16, 128), vm(1024, 384),
            dma(2), dma(4), dma(2, 2), dma(2, 2), dma(16), dma(16), dma(8), dma(8), dma(8), dma(8),
            dma(16), dma(16), dma(16), dma(16), dma(8), dma(8), dma(8), dma(8), dma(8), dma(8),
            dma(16), dma(16), dma(16), dma(16),
        ],
        compiler_params=pltpu.CompilerParams(
            collective_id=0, has_side_effects=True, vmem_limit_bytes=60 << 20
        ),
        name="pair_backward",
    )(
        pair_repr, logit_cotangent, pair_mask, single_repr, token_index.reshape(8, 128), token_index,
        pair_up, pair_gate, pair_down, head_weight, rel_table, proj_row, proj_col,
        single_gate, single_up, single_down,
    )


def solution(mesh):
    strip = P(("row", "col"), None)
    return jax.shard_map(
        local,
        mesh=mesh,
        in_specs=(P("row", "col", None), P("row", "col", None), P("row", "col"), strip) + (P(),) * 11,
        out_specs=(P("row", "col", None), strip) + (P(),) * 7
        + (P(None, ("row", "col")), P(None, ("row", "col")), strip),
        check_vma=False,
    )
```

```python
import jax
import jax.numpy as jnp
from jax import lax
from jax.experimental import pallas as pl
from jax.experimental.pallas import tpu as pltpu
from jax.sharding import PartitionSpec as P

F = jnp.float32
B = jnp.bfloat16
MESH = pl.DeviceIdType.MESH
NR, NC = 8, 16
EPS = 1e-05
BR = 32
SHARE = 112


def mm(a, b):
    return lax.dot_general(a, b, (((1,), (0,)), ((), ())), preferred_element_type=F)


def nt(a, b):
    return lax.dot_general(a, b, (((1,), (1,)), ((), ())), preferred_element_type=F)


def tn(a, b):
    return lax.dot_general(a, b, (((0,), (0,)), ((), ())), preferred_element_type=F)


def sigmoid(v):
    return 0.5 * jnp.tanh(0.5 * v) + 0.5


def local_wait(ref, sem):
    pltpu.make_async_copy(ref, ref, sem).wait()


def kernel(
    pair_hbm, cot_hbm, mask, single, tok, tok_s, up, gate, down, head, rel, prow, pcol,
    sgate_hbm, sup_hbm, sdown_hbm,
    og, osg, oup, ogate, odown, ohead, orel, opr, opc, osgate, osup, osdown,
    pairv, cotv, ogv, lo, hi, pos, srel, smask, tbuf, sendm, mirb, sb, rowp, colp,
    arow, acol, aug, adn, ahd, arl, ws, wr, w2, w3, rr, cr, tb, cots,
    sgate, sup, sdown, pieces, nball, uall, si12, slope12, h12, own_down,
    in_sem, out_sem, msend, mrecv, gsend, grecv, csend, crecv, hsend, hrecv, bsend, brecv, qsend, qrecv,
    p1s, p1r, rs1, rr1, cs1, cr1, p2s, p2r, t2s, t2r, p3s, p3r, t3s, t3r,
):
    r = lax.axis_index("row")
    c = lax.axis_index("col")
    joint = r * NC + c
    diag = c // 2 == r

    cot_in = pltpu.make_async_copy(cot_hbm, cotv, in_sem.at[0])
    cot_in.start()
    pair_in = pltpu.make_async_copy(pair_hbm, pairv, in_sem.at[1])
    weights_in = [
        pltpu.make_async_copy(a, b, in_sem.at[2 + k])
        for k, (a, b) in enumerate(((sgate_hbm, sgate), (sup_hbm, sup), (sdown_hbm, sdown)))
    ]
    for cp in weights_in:
        cp.start()
    pair_in.start()

    bar = pltpu.get_barrier_semaphore()
    for d in range(1, NC):
        pl.semaphore_signal(bar, inc=1, device_id=(r, lax.rem(c + d, NC)), device_id_type=MESH)
    for d in range(1, NR):
        pl.semaphore_signal(bar, inc=1, device_id=(lax.rem(r + d, NR), c), device_id_type=MESH)
    for h in range(2):
        @pl.when(jnp.logical_not(jnp.logical_and(diag, c % 2 == h)))
        def _():
            pl.semaphore_signal(bar, inc=1, device_id=(c // 2, 2 * r + h), device_id_type=MESH)

    lane = lax.broadcasted_iota(jnp.int32, (64, 128), 1)
    trow = jnp.broadcast_to(tok[pl.ds(c // 2, 1), :].astype(F), (128, 128))
    pos[...] = jnp.transpose(trow)
    e = pos[pl.ds((c % 2) * 64, 64), :].astype(jnp.int32) + lane - 32
    big = jnp.int32(1 << 20)
    lo[...] = jnp.where(lane == 0, -big, jnp.where(lane > 64, big, e))
    hi[...] = jnp.where(lane == 64, big, jnp.where(lane > 64, -big, e))
    srel[...] = jnp.zeros_like(srel)
    srel[0:65, :] = rel[...].astype(F)
    mt = mask[...].astype(F)
    for b in range(4):
        smask[b] = mt[:, b * 32:(b + 1) * 32]
    for a in (acol, aug, adn, ahd, arl):
        a[...] = jnp.zeros_like(a)

    pl.semaphore_wait(bar, NC + NR - jnp.where(diag, 1, 0))

    def col_copies(src_ref, dst_ref, ss, rs):
        return [
            pltpu.make_async_remote_copy(
                src_ref=src_ref(lax.rem(c + d, NC)), dst_ref=dst_ref, send_sem=ss.at[d], recv_sem=rs.at[d],
                device_id=(r, lax.rem(c + d, NC)), device_id_type=MESH,
            )
            for d in range(1, NC)
        ]

    def row_copies(src_ref, dst_ref, ss, rs):
        return [
            pltpu.make_async_remote_copy(
                src_ref=src_ref(lax.rem(r + d, NR)), dst_ref=dst_ref, send_sem=ss.at[d], recv_sem=rs.at[d],
                device_id=(lax.rem(r + d, NR), c), device_id_type=MESH,
            )
            for d in range(1, NR)
        ]

    def start(copies):
        for cp in copies:
            cp.start()

    def wait(copies):
        for cp in copies:
            cp.wait()

    def sent_mirror(t):
        for h in range(2):
            @pl.when(jnp.logical_not(jnp.logical_and(diag, c % 2 == h)))
            def _():
                local_wait(sendm.at[t, h], msend.at[t, h])

    src = single[...].astype(F)
    sb[r, c, 0] = jnp.concatenate([src[:, :128], src[:, 128:256]], axis=0).astype(B)
    sb[r, c, 1] = jnp.concatenate([src[:, 256:], src[:, 256:]], axis=0).astype(B)
    strips = col_copies(lambda j: sb.at[r, c], sb.at[r, c], gsend, grecv)
    start(strips)

    cot_in.wait()
    half_lane = lax.broadcasted_iota(jnp.int32, (16, 128), 1) < 64
    for h in range(2):
        @pl.loop(0, 2)
        def _(b):
            p0 = h * 64 + b * 32
            sm = smask[2 * h + b]
            for i in range(32):
                v = cotv[p0 + i].astype(F) * jnp.broadcast_to(sm[:, i:i + 1], (64, 128))
                cotv[p0 + i] = v.astype(B)
                for t in range(2):
                    first = pltpu.roll(v[32 * t:32 * t + 16], 64, 1)
                    second = v[32 * t + 16:32 * t + 32]
                    at = pl.multiple_of((b * 32 + i) * 16, 16)
                    tbuf[t, pl.ds(at, 16), :] = jnp.where(half_lane, first, second)
        for t in range(2):
            for k in range(16):
                sendm[t, h, k] = tbuf[t, pl.ds(k, 64, stride=16), :].astype(B)
    def send_mirror(t):
        for h in range(2):
            own = jnp.logical_and(diag, c % 2 == h)

            @pl.when(own)
            def _():
                pltpu.make_async_copy(sendm.at[t, h], mirb.at[c % 2, t], mrecv.at[c % 2, t]).start()

            @pl.when(jnp.logical_not(own))
            def _():
                pltpu.make_async_remote_copy(
                    src_ref=sendm.at[t, h], dst_ref=mirb.at[c % 2, t], send_sem=msend.at[t, h],
                    recv_sem=mrecv.at[c % 2, t], device_id=(c // 2, 2 * r + h), device_id_type=MESH,
                ).start()

    send_mirror(0)

    for cp in weights_in:
        cp.wait()
    inv_rms = lax.rsqrt(jnp.mean(src * src, axis=-1, keepdims=True) + EPS)
    normed = src * inv_rms
    nbf = normed.astype(B)
    s_gate = mm(nbf, sgate[...])
    s_up = mm(nbf, sup[...])
    s_sig = sigmoid(s_gate)
    s_silu = s_gate * s_sig
    s_hid = (s_silu * s_up).astype(B)
    updated = (src + mm(s_hid, sdown[...])).astype(B)
    row_piece = mm(updated, prow[...])
    col_piece = mm(updated, pcol[...])
    pieces[c] = jnp.concatenate([row_piece, col_piece], axis=0).astype(B)
    projected = col_copies(lambda j: pieces.at[c], pieces.at[c], qsend, qrecv)
    start(projected)

    half = pl.ds(pl.multiple_of((c % 2) * 8, 8), 8)
    wait(strips)
    spread = row_copies(lambda j: sb.at[r, half], sb.at[r, half], hsend, hrecv)
    start(spread)

    wait(projected)
    both = pieces[...].astype(F)
    rowp[...] = both[:, :8].reshape(128, 128)
    cols = row_copies(lambda j: colp, colp, csend, crecv)

    @pl.when(diag)
    def _():
        pos[...] = both[:, 8:].reshape(128, 128)
        colp[...] = pos[pl.ds((c % 2) * 64, 64), :].astype(B)
        start(cols)

    def to_sibling(d):
        rows = sb.at[lax.rem(r + NR - d, NR), half]
        return pltpu.make_async_remote_copy(
            src_ref=rows, dst_ref=rows, send_sem=bsend.at[d], recv_sem=brecv.at[d],
            device_id=(r, c + 1 - 2 * (c % 2)), device_id_type=MESH,
        )

    @pl.when(jnp.logical_not(diag))
    def _():
        for d in range(1, NR):
            @pl.when(lax.rem(c // 2 + d, NR) == r)
            def _():
                local_wait(colp, crecv.at[d])

    @pl.when(diag)
    def _():
        for cp in cols:
            cp.wait_send()

    wait(spread)
    for d in range(1, NR):
        to_sibling(d).start()
    sent_mirror(0)
    send_mirror(1)

    def every_token():
        picks = lax.broadcasted_iota(jnp.int32, (128, 1536), 1)
        unit = lax.broadcasted_iota(jnp.int32, (128, 1536), 0)
        pick = jnp.where((picks == joint * 12 + unit) & (unit < 12), F(1), F(0)).astype(B)
        own_gate = nt(pick, sgate[...]).astype(B)
        own_up = nt(pick, sup[...]).astype(B)
        own_down[...] = mm(pick, sdown[...]).astype(B)

        @pl.loop(0, 4)
        def _(q):
            rows = pl.ds(pl.multiple_of(q * 256, 256), 256)
            v = sb[pl.ds(q * 2, 2)].astype(F)
            s_all = jnp.concatenate(
                [
                    v[:, :, 0, :8].reshape(256, 128), v[:, :, 0, 8:].reshape(256, 128),
                    v[:, :, 1, :8].reshape(256, 128),
                ],
                axis=1,
            )
            nb = (s_all * lax.rsqrt(jnp.mean(s_all * s_all, axis=-1, keepdims=True) + EPS)).astype(B)
            nball[rows] = nb
            gate_all = mm(nb, sgate[...])
            hid_all = (gate_all * sigmoid(gate_all) * mm(nb, sup[...])).astype(B)
            uall[rows] = (s_all + mm(hid_all, sdown[...])).astype(B)
            g12 = nt(nb, own_gate)
            u12 = nt(nb, own_up)
            sg12 = sigmoid(g12)
            silu = g12 * sg12
            si12[rows] = silu
            slope12[rows] = u12 * (sg12 + silu * (1.0 - sg12))
            h12[rows] = (silu * u12).astype(B)

    pair_in.wait()
    lane3 = lax.broadcasted_iota(jnp.int32, (1, 1, 128), 2)

    @pl.loop(0, 4)
    def _(b):
        s = b % 2
        t = b // 2
        i0 = pl.multiple_of(s * 64 + t * 32, 32)
        local_wait(mirb.at[s, t], mrecv.at[s, t])
        m = BR * 64
        hots = []
        for k in range(BR):
            at = tok_s[r * 128 + i0 + k]
            hots.append(jnp.where((lo[...] <= at) & (hi[...] >= at), F(1), F(0)).astype(B))
        hot = jnp.concatenate(hots, axis=0)
        x = (
            pairv[pl.ds(i0, BR)].astype(F)
            + rowp[pl.ds(i0, BR)][:, None, :]
            + colp[...].astype(F)[None]
        )
        x = x.reshape(m, 128) + mm(hot, srel[...].astype(B))
        cen = x - jnp.mean(x, axis=-1, keepdims=True)
        inv = lax.rsqrt(jnp.mean(cen * cen, axis=-1, keepdims=True) + EPS)
        nm = cen * inv
        nb = nm.astype(B)
        u = mm(nb, up[...])
        g = mm(nb, gate[...])
        sg = sigmoid(g)
        si = g * sg
        hid = (si * u).astype(B)
        po = (x + mm(hid, down[...])).astype(B)
        mv = mirb[s, t].astype(F)
        first = pltpu.roll(mv.reshape(1024, 128), 64, 1).reshape(16, 64, 128)
        mir = jnp.where(lane3 >= 64, jnp.concatenate([first, mv], axis=0), 0.0)
        hc = (cotv[pl.ds(i0, BR)].astype(F) + mir).astype(B).reshape(m, 128)
        go = nt(hc, head[...])
        gb = go.astype(B)
        gh = nt(gb, down[...])
        gu = (gh * si).astype(B)
        gg = (gh * u * (sg + si * (1.0 - sg))).astype(B)
        gn = nt(gu, up[...]) + nt(gg, gate[...])
        gx = go + inv * (
            gn - jnp.mean(gn, axis=-1, keepdims=True) - nm * jnp.mean(gn * nm, axis=-1, keepdims=True)
        )
        gt = gx.reshape(BR, 64, 128)
        gxb = gx.astype(B)
        ogv[pl.ds(i0, BR)] = gxb.reshape(BR, 64, 128)
        pltpu.make_async_copy(ogv.at[pl.ds(i0, BR)], og.at[pl.ds(i0, BR)], out_sem.at[b]).start()
        arow[pl.ds(i0, BR)] = jnp.sum(gt, axis=1)
        acol[...] += jnp.sum(gt, axis=0)
        aug[:, :512] += tn(nb, gu)
        aug[:, 512:] += tn(nb, gg)
        adn[...] += tn(gb, hid)
        ahd[...] += tn(po, hc)
        arl[...] += tn(hot, gxb)

        @pl.when(b == 1)
        def _():
            for d in range(1, NR):
                to_sibling(d).wait()
            every_token()

    for k in range(8):
        ws[k * 128:(k + 1) * 128] = aug[:, k * 128:(k + 1) * 128].astype(B)
    for k in range(4):
        ws[1024 + k * 128:1152 + k * 128] = adn[:, k * 128:(k + 1) * 128].astype(B)
    ws[1536:1664] = ahd[...].astype(B)
    ws[1664:1792] = arl[...].astype(B)
    share = lambda j: pl.ds(pl.multiple_of(j * SHARE, 16), SHARE)
    strip = lambda j: pl.ds(pl.multiple_of(j * 8, 8), 8)
    s_row = col_copies(lambda j: arow.at[strip(j)], rr.at[c], rs1, rr1)
    s_col = row_copies(lambda j: acol.at[strip(j)], cr.at[r], cs1, cr1)
    s_w = col_copies(lambda j: ws.at[share(j)], wr.at[c], p1s, p1r)
    start(s_row)
    start(s_col)
    start(s_w)
    wr[c] = ws[share(c)]
    rr[c] = arow[strip(c)]
    cr[r] = acol[strip(r)]

    wait(s_row)
    wait(s_col)
    row_own = rr[0]
    for k in range(1, NC):
        row_own = row_own + rr[k]
    col_own = cr[0]
    for k in range(1, NR):
        col_own = col_own + cr[k]
    tb[c, r] = jnp.concatenate([row_own, col_own], axis=0).astype(B)
    t2 = row_copies(lambda j: tb.at[c, r], tb.at[c, r], t2s, t2r)
    start(t2)
    wait(s_w)
    w = wr[0].astype(F)
    for k in range(1, NC):
        w = w + wr[k].astype(F)
    w2[r] = w.astype(B)
    s2 = row_copies(lambda j: w2.at[r], w2.at[r], p2s, p2r)
    start(s2)
    wait(t2)
    t3 = col_copies(lambda j: tb.at[c], tb.at[c], t3s, t3r)
    start(t3)
    wait(s2)
    w = w2[0].astype(F)
    for k in range(1, NR):
        w = w + w2[k].astype(F)
    w3[share(c)] = w.astype(B)
    s3 = col_copies(lambda j: w3.at[share(c)], w3.at[share(c)], p3s, p3r)
    start(s3)

    scale = 1.0 / 1024
    wait(t3)
    tf = tb[...].astype(F)
    row_all = jnp.swapaxes(tf[:, :, :8], 0, 1).reshape(1024, 128).astype(B)
    col_all = tf[:, :, 8:].reshape(1024, 128).astype(B)
    cot_all = nt(row_all, prow[...]) + nt(col_all, pcol[...])
    cots[...] = cot_all
    cb = cot_all.astype(B)
    gsh = nt(cb, own_down[...])
    gsu = (gsh * si12[...]).astype(B)
    gsg = (gsh * slope12[...]).astype(B)
    osgate[...] = tn(gsg, nball[...])[:12] * scale
    osup[...] = tn(gsu, nball[...])[:12] * scale
    osdown[...] = tn(h12[...], cb)[:12] * scale
    opr[...] = tn(uall[...], row_all) * scale
    opc[...] = tn(uall[...], col_all) * scale
    c8 = cots[pl.ds(pl.multiple_of(joint * 8, 8), 8), :]
    g8 = nt(c8.astype(B), sdown[...])
    gu8 = (g8 * s_silu).astype(B)
    gg8 = (g8 * s_up * (s_sig + s_silu * (1.0 - s_sig))).astype(B)
    gn8 = nt(gg8, sgate[...]) + nt(gu8, sup[...])
    osg[...] = (
        c8 + inv_rms * (gn8 - normed * jnp.mean(gn8 * normed, axis=-1, keepdims=True))
    ).astype(B)

    wait(s3)
    for k in range(4):
        ks = slice(k * 128, (k + 1) * 128)
        oup[:, ks] = w3[k * 128:(k + 1) * 128].astype(F) * scale
        ogate[:, ks] = w3[512 + k * 128:640 + k * 128].astype(F) * scale
        odown[ks, :] = jnp.transpose(w3[1024 + k * 128:1152 + k * 128].astype(F)) * scale
    ohead[...] = w3[1536:1664].astype(F) * scale
    orel[...] = (w3[1664:1792].astype(F) * scale)[:65]

    sent_mirror(1)
    for b in range(4):
        i0 = (b % 2) * 64 + (b // 2) * 32
        pltpu.make_async_copy(ogv.at[pl.ds(i0, BR)], og.at[pl.ds(i0, BR)], out_sem.at[b]).wait()


def hand_over(*refs):
    ins, outs, held, sem_in, sem_out = refs[:12], refs[12:24], refs[24:36], refs[36], refs[37]
    parts = []
    for k in range(12):
        if k == 0:
            parts += [(k, pl.ds(p * 32, 32)) for p in range(4)]
        else:
            parts += [(k, slice(None))]
    into = [
        pltpu.make_async_copy(ins[k].at[rows], held[k].at[rows], sem_in.at[n])
        for n, (k, rows) in enumerate(parts)
    ]
    out = [
        pltpu.make_async_copy(held[k].at[rows], outs[k].at[rows], sem_out.at[n])
        for n, (k, rows) in enumerate(parts)
    ]
    for cp in into:
        cp.start()
    for a, b in zip(into, out):
        a.wait()
        b.start()
    for cp in out:
        cp.wait()


def local(
    pair_repr, logit_cotangent, pair_mask, single_repr, token_index, pair_up, pair_gate, pair_down,
    head_weight, rel_table, proj_row, proj_col, single_gate, single_up, single_down,
):
    S = lambda shape, dtype=F: jax.ShapeDtypeStruct(shape, dtype)
    V = pl.BlockSpec(memory_space=pltpu.VMEM)
    H = pl.BlockSpec(memory_space=pl.ANY)
    vm = lambda *shape: pltpu.VMEM(shape, F)
    vb = lambda *shape: pltpu.VMEM(shape, B)
    dma = lambda *shape: pltpu.SemaphoreType.DMA(shape)
    outs = pl.pallas_call(
        kernel,
        out_shape=(
            S((128, 64, 128), B), S((8, 384), B), S((128, 512)), S((128, 512)), S((512, 128)),
            S((128, 128)), S((65, 128)), S((384, 128)), S((384, 128)), S((12, 384)), S((12, 384)),
            S((12, 384)),
        ),
        in_specs=[H, H, V, V, V, pl.BlockSpec(memory_space=pltpu.SMEM)] + [V] * 7 + [H] * 3,
        out_specs=[H] + [V] * 11,
        scratch_shapes=[
            vb(128, 64, 128), vb(128, 64, 128), vb(128, 64, 128),
            pltpu.VMEM((64, 128), jnp.int32), pltpu.VMEM((64, 128), jnp.int32), vm(128, 128), vm(128, 128),
            vm(4, 64, 32), vm(2, 1024, 128), vb(2, 2, 16, 64, 128), vb(2, 2, 16, 64, 128),
            vb(8, 16, 2, 16, 128), vm(128, 128), vb(64, 128),
            vm(128, 128), vm(64, 128), vm(128, 1024), vm(128, 512), vm(128, 128), vm(128, 128),
            vb(1792, 128), vb(16, SHARE, 128), vb(8, SHARE, 128), vb(1792, 128),
            vm(16, 8, 128), vm(8, 8, 128), vb(16, 8, 16, 128), vm(1024, 384),
            vb(384, 1536), vb(384, 1536), vb(1536, 384), vb(16, 16, 128), vb(1024, 384), vb(1024, 384),
            vm(1024, 128), vm(1024, 128), vb(1024, 128), vb(128, 384),
            dma(5), dma(4), dma(2, 2), dma(2, 2), dma(16), dma(16), dma(8), dma(8), dma(8), dma(8), dma(8),
            dma(8), dma(16), dma(16),
            dma(16), dma(16), dma(16), dma(16), dma(8), dma(8), dma(8), dma(8), dma(8), dma(8),
            dma(16), dma(16), dma(16), dma(16),
        ],
        compiler_params=pltpu.CompilerParams(
            collective_id=0, has_side_effects=True, vmem_limit_bytes=60 << 20
        ),
        name="pair_backward",
    )(
        pair_repr, logit_cotangent, pair_mask.T, single_repr, token_index.reshape(8, 128), token_index,
        pair_up, pair_gate, pair_down, head_weight, rel_table, proj_row, proj_col,
        single_gate, single_up, single_down,
    )
    outs = pl.pallas_call(
        hand_over,
        out_shape=[S(o.shape, o.dtype) for o in outs],
        in_specs=[H] * 12,
        out_specs=[H] * 12,
        scratch_shapes=[pltpu.VMEM(o.shape, o.dtype) for o in outs] + [dma(15), dma(15)],
        name="hand_over",
    )(*outs)
    return (*outs[:9], outs[9].T, outs[10].T, outs[11])


def solution(mesh):
    strip = P(("row", "col"), None)
    return jax.shard_map(
        local,
        mesh=mesh,
        in_specs=(P("row", "col", None), P("row", "col", None), P("row", "col"), strip) + (P(),) * 11,
        out_specs=(P("row", "col", None), strip) + (P(),) * 7
        + (P(None, ("row", "col")), P(None, ("row", "col")), strip),
        check_vma=False,
    )
```

```python
import jax
import jax.numpy as jnp
from jax import lax
from jax.experimental import pallas as pl
from jax.experimental.pallas import tpu as pltpu
from jax.sharding import PartitionSpec as P

F = jnp.float32
B = jnp.bfloat16
MESH = pl.DeviceIdType.MESH
NR, NC = 8, 16
EPS = 1e-05
BR = 32
SHARE = 112


def mm(a, b):
    return lax.dot_general(a, b, (((1,), (0,)), ((), ())), preferred_element_type=F)


def nt(a, b):
    return lax.dot_general(a, b, (((1,), (1,)), ((), ())), preferred_element_type=F)


def tn(a, b):
    return lax.dot_general(a, b, (((0,), (0,)), ((), ())), preferred_element_type=F)


def sigmoid(v):
    return 0.5 * jnp.tanh(0.5 * v) + 0.5


def local_wait(ref, sem):
    pltpu.make_async_copy(ref, ref, sem).wait()


def kernel(
    pair_hbm, cot_hbm, mask, single, tok, tok_s, up, gate, down, head, rel, prow, pcol,
    sgate_hbm, sup_hbm, sdown_hbm,
    og, osg, oup, ogate, odown, ohead, orel, opr, opc, osgate, osup, osdown,
    pairv, cotv, ogv, lo, hi, pos, srel, smask, tbuf, sendm, mirb, sb, rowp, colp,
    arow, acol, aug, adn, ahd, arl, ws, wr, w2, w3, rr, cr, tb, cots,
    sgate, sup, sdown, pieces, nball, uall, si12, slope12, h12, own_down,
    in_sem, out_sem, msend, mrecv, gsend, grecv, csend, crecv, hsend, hrecv, bsend, brecv, qsend, qrecv,
    p1s, p1r, rs1, rr1, cs1, cr1, p2s, p2r, t2s, t2r, p3s, p3r, t3s, t3r,
):
    r = lax.axis_index("row")
    c = lax.axis_index("col")
    joint = r * NC + c
    diag = c // 2 == r

    cot_in = pltpu.make_async_copy(cot_hbm, cotv, in_sem.at[0])
    cot_in.start()
    pair_in = pltpu.make_async_copy(pair_hbm, pairv, in_sem.at[1])
    weights_in = [
        pltpu.make_async_copy(a, b, in_sem.at[2 + k])
        for k, (a, b) in enumerate(((sgate_hbm, sgate), (sup_hbm, sup), (sdown_hbm, sdown)))
    ]
    for cp in weights_in:
        cp.start()
    pair_in.start()

    bar = pltpu.get_barrier_semaphore()
    for d in range(1, NC):
        pl.semaphore_signal(bar, inc=1, device_id=(r, lax.rem(c + d, NC)), device_id_type=MESH)
    for d in range(1, NR):
        pl.semaphore_signal(bar, inc=1, device_id=(lax.rem(r + d, NR), c), device_id_type=MESH)
    for h in range(2):
        @pl.when(jnp.logical_not(jnp.logical_and(diag, c % 2 == h)))
        def _():
            pl.semaphore_signal(bar, inc=1, device_id=(c // 2, 2 * r + h), device_id_type=MESH)

    lane = lax.broadcasted_iota(jnp.int32, (64, 128), 1)
    trow = jnp.broadcast_to(tok[pl.ds(c // 2, 1), :].astype(F), (128, 128))
    pos[...] = jnp.transpose(trow)
    e = pos[pl.ds((c % 2) * 64, 64), :].astype(jnp.int32) + lane - 32
    big = jnp.int32(1 << 20)
    lo[...] = jnp.where(lane == 0, -big, jnp.where(lane > 64, big, e))
    hi[...] = jnp.where(lane == 64, big, jnp.where(lane > 64, -big, e))
    srel[...] = jnp.zeros_like(srel)
    srel[0:65, :] = rel[...].astype(F)
    mt = mask[...].astype(F)
    for b in range(4):
        smask[b] = mt[:, b * 32:(b + 1) * 32]
    for a in (acol, aug, adn, ahd, arl):
        a[...] = jnp.zeros_like(a)

    pl.semaphore_wait(bar, NC + NR - jnp.where(diag, 1, 0))

    def col_copies(src_ref, dst_ref, ss, rs):
        return [
            pltpu.make_async_remote_copy(
                src_ref=src_ref(lax.rem(c + d, NC)), dst_ref=dst_ref, send_sem=ss.at[d], recv_sem=rs.at[d],
                device_id=(r, lax.rem(c + d, NC)), device_id_type=MESH,
            )
            for d in range(1, NC)
        ]

    def row_copies(src_ref, dst_ref, ss, rs):
        return [
            pltpu.make_async_remote_copy(
                src_ref=src_ref(lax.rem(r + d, NR)), dst_ref=dst_ref, send_sem=ss.at[d], recv_sem=rs.at[d],
                device_id=(lax.rem(r + d, NR), c), device_id_type=MESH,
            )
            for d in range(1, NR)
        ]

    def start(copies):
        for cp in copies:
            cp.start()

    def wait(copies):
        for cp in copies:
            cp.wait()

    def sent_mirror(t):
        for h in range(2):
            @pl.when(jnp.logical_not(jnp.logical_and(diag, c % 2 == h)))
            def _():
                local_wait(sendm.at[t, h], msend.at[t, h])

    src = single[...].astype(F)
    sb[r, c, 0] = jnp.concatenate([src[:, :128], src[:, 128:256]], axis=0).astype(B)
    sb[r, c, 1] = jnp.concatenate([src[:, 256:], src[:, 256:]], axis=0).astype(B)
    strips = col_copies(lambda j: sb.at[r, c], sb.at[r, c], gsend, grecv)
    start(strips)

    def send_mirror(t, h):
        own = jnp.logical_and(diag, c % 2 == h)

        @pl.when(own)
        def _():
            pltpu.make_async_copy(sendm.at[t, h], mirb.at[c % 2, t], mrecv.at[c % 2, t]).start()

        @pl.when(jnp.logical_not(own))
        def _():
            pltpu.make_async_remote_copy(
                src_ref=sendm.at[t, h], dst_ref=mirb.at[c % 2, t], send_sem=msend.at[t, h],
                recv_sem=mrecv.at[c % 2, t], device_id=(c // 2, 2 * r + h), device_id_type=MESH,
            ).start()

    half = pl.ds(pl.multiple_of((c % 2) * 8, 8), 8)
    spread = row_copies(lambda j: sb.at[r, half], sb.at[r, half], hsend, hrecv)

    cot_in.wait()
    half_lane = lax.broadcasted_iota(jnp.int32, (16, 128), 1) < 64
    for h in range(2):
        @pl.loop(0, 2)
        def _(b):
            p0 = h * 64 + b * 32
            sm = smask[2 * h + b]
            for i in range(32):
                v = cotv[p0 + i].astype(F) * jnp.broadcast_to(sm[:, i:i + 1], (64, 128))
                cotv[p0 + i] = v.astype(B)
                for t in range(2):
                    first = pltpu.roll(v[32 * t:32 * t + 16], 64, 1)
                    second = v[32 * t + 16:32 * t + 32]
                    at = pl.multiple_of((b * 32 + i) * 16, 16)
                    tbuf[t, pl.ds(at, 16), :] = jnp.where(half_lane, first, second)
        for t in range(2):
            for k in range(16):
                sendm[t, h, k] = tbuf[t, pl.ds(k, 64, stride=16), :].astype(B)
        if h == 0:
            wait(strips)
            start(spread)
        send_mirror(0, h)
    for cp in weights_in:
        cp.wait()
    inv_rms = lax.rsqrt(jnp.mean(src * src, axis=-1, keepdims=True) + EPS)
    normed = src * inv_rms
    nbf = normed.astype(B)
    s_gate = mm(nbf, sgate[...])
    s_up = mm(nbf, sup[...])
    s_sig = sigmoid(s_gate)
    s_silu = s_gate * s_sig
    s_hid = (s_silu * s_up).astype(B)
    updated = (src + mm(s_hid, sdown[...])).astype(B)
    row_piece = mm(updated, prow[...])
    col_piece = mm(updated, pcol[...])
    pieces[c] = jnp.concatenate([row_piece, col_piece], axis=0).astype(B)
    projected = col_copies(lambda j: pieces.at[c], pieces.at[c], qsend, qrecv)
    start(projected)

    wait(projected)
    both = pieces[...].astype(F)
    rowp[...] = both[:, :8].reshape(128, 128)
    cols = row_copies(lambda j: colp, colp, csend, crecv)

    @pl.when(diag)
    def _():
        pos[...] = both[:, 8:].reshape(128, 128)
        colp[...] = pos[pl.ds((c % 2) * 64, 64), :].astype(B)
        start(cols)

    def to_sibling(d):
        rows = sb.at[lax.rem(r + NR - d, NR), half]
        return pltpu.make_async_remote_copy(
            src_ref=rows, dst_ref=rows, send_sem=bsend.at[d], recv_sem=brecv.at[d],
            device_id=(r, c + 1 - 2 * (c % 2)), device_id_type=MESH,
        )

    @pl.when(jnp.logical_not(diag))
    def _():
        for d in range(1, NR):
            @pl.when(lax.rem(c // 2 + d, NR) == r)
            def _():
                local_wait(colp, crecv.at[d])

    @pl.when(diag)
    def _():
        for cp in cols:
            cp.wait_send()

    wait(spread)
    for d in range(1, NR):
        to_sibling(d).start()
    sent_mirror(0)
    send_mirror(1, 0)
    send_mirror(1, 1)

    def every_token():
        picks = lax.broadcasted_iota(jnp.int32, (128, 1536), 1)
        unit = lax.broadcasted_iota(jnp.int32, (128, 1536), 0)
        pick = jnp.where((picks == joint * 12 + unit) & (unit < 12), F(1), F(0)).astype(B)
        own_gate = nt(pick, sgate[...]).astype(B)
        own_up = nt(pick, sup[...]).astype(B)
        own_down[...] = mm(pick, sdown[...]).astype(B)

        @pl.loop(0, 4)
        def _(q):
            rows = pl.ds(pl.multiple_of(q * 256, 256), 256)
            v = sb[pl.ds(q * 2, 2)].astype(F)
            s_all = jnp.concatenate(
                [
                    v[:, :, 0, :8].reshape(256, 128), v[:, :, 0, 8:].reshape(256, 128),
                    v[:, :, 1, :8].reshape(256, 128),
                ],
                axis=1,
            )
            nb = (s_all * lax.rsqrt(jnp.mean(s_all * s_all, axis=-1, keepdims=True) + EPS)).astype(B)
            nball[rows] = nb
            gate_all = mm(nb, sgate[...])
            hid_all = (gate_all * sigmoid(gate_all) * mm(nb, sup[...])).astype(B)
            uall[rows] = (s_all + mm(hid_all, sdown[...])).astype(B)
            g12 = nt(nb, own_gate)
            u12 = nt(nb, own_up)
            sg12 = sigmoid(g12)
            silu = g12 * sg12
            si12[rows] = silu
            slope12[rows] = u12 * (sg12 + silu * (1.0 - sg12))
            h12[rows] = (silu * u12).astype(B)

    pair_in.wait()
    lane3 = lax.broadcasted_iota(jnp.int32, (1, 1, 128), 2)

    @pl.loop(0, 4)
    def _(b):
        s = b % 2
        t = b // 2
        i0 = pl.multiple_of(s * 64 + t * 32, 32)
        local_wait(mirb.at[s, t], mrecv.at[s, t])
        m = BR * 64
        hots = []
        for k in range(BR):
            at = tok_s[r * 128 + i0 + k]
            hots.append(jnp.where((lo[...] <= at) & (hi[...] >= at), F(1), F(0)).astype(B))
        hot = jnp.concatenate(hots, axis=0)
        x = (
            pairv[pl.ds(i0, BR)].astype(F)
            + rowp[pl.ds(i0, BR)][:, None, :]
            + colp[...].astype(F)[None]
        )
        x = x.reshape(m, 128) + mm(hot, srel[...].astype(B))
        cen = x - jnp.mean(x, axis=-1, keepdims=True)
        inv = lax.rsqrt(jnp.mean(cen * cen, axis=-1, keepdims=True) + EPS)
        nm = cen * inv
        nb = nm.astype(B)
        u = mm(nb, up[...])
        g = mm(nb, gate[...])
        sg = sigmoid(g)
        si = g * sg
        hid = (si * u).astype(B)
        po = (x + mm(hid, down[...])).astype(B)
        mv = mirb[s, t].astype(F)
        first = pltpu.roll(mv.reshape(1024, 128), 64, 1).reshape(16, 64, 128)
        mir = jnp.where(lane3 >= 64, jnp.concatenate([first, mv], axis=0), 0.0)
        hc = (cotv[pl.ds(i0, BR)].astype(F) + mir).astype(B).reshape(m, 128)
        go = nt(hc, head[...])
        gb = go.astype(B)
        gh = nt(gb, down[...])
        gu = (gh * si).astype(B)
        gg = (gh * u * (sg + si * (1.0 - sg))).astype(B)
        gn = nt(gu, up[...]) + nt(gg, gate[...])
        gx = go + inv * (
            gn - jnp.mean(gn, axis=-1, keepdims=True) - nm * jnp.mean(gn * nm, axis=-1, keepdims=True)
        )
        gt = gx.reshape(BR, 64, 128)
        gxb = gx.astype(B)
        ogv[pl.ds(i0, BR)] = gxb.reshape(BR, 64, 128)
        pltpu.make_async_copy(ogv.at[pl.ds(i0, BR)], og.at[pl.ds(i0, BR)], out_sem.at[b]).start()
        arow[pl.ds(i0, BR)] = jnp.sum(gt, axis=1)
        acol[...] += jnp.sum(gt, axis=0)
        aug[:, :512] += tn(nb, gu)
        aug[:, 512:] += tn(nb, gg)
        adn[...] += tn(gb, hid)
        ahd[...] += tn(po, hc)
        arl[...] += tn(hot, gxb)

        @pl.when(b == 1)
        def _():
            for d in range(1, NR):
                to_sibling(d).wait()
            every_token()

    for k in range(8):
        ws[k * 128:(k + 1) * 128] = aug[:, k * 128:(k + 1) * 128].astype(B)
    for k in range(4):
        ws[1024 + k * 128:1152 + k * 128] = adn[:, k * 128:(k + 1) * 128].astype(B)
    ws[1536:1664] = ahd[...].astype(B)
    ws[1664:1792] = arl[...].astype(B)
    share = lambda j: pl.ds(pl.multiple_of(j * SHARE, 16), SHARE)
    strip = lambda j: pl.ds(pl.multiple_of(j * 8, 8), 8)
    s_row = col_copies(lambda j: arow.at[strip(j)], rr.at[c], rs1, rr1)
    s_col = row_copies(lambda j: acol.at[strip(j)], cr.at[r], cs1, cr1)
    s_w = col_copies(lambda j: ws.at[share(j)], wr.at[c], p1s, p1r)
    start(s_row)
    start(s_col)
    start(s_w)
    wr[c] = ws[share(c)]
    rr[c] = arow[strip(c)]
    cr[r] = acol[strip(r)]

    wait(s_row)
    wait(s_col)
    row_own = rr[0]
    for k in range(1, NC):
        row_own = row_own + rr[k]
    col_own = cr[0]
    for k in range(1, NR):
        col_own = col_own + cr[k]
    tb[c, r] = jnp.concatenate([row_own, col_own], axis=0).astype(B)
    t2 = row_copies(lambda j: tb.at[c, r], tb.at[c, r], t2s, t2r)
    start(t2)
    wait(s_w)
    w = wr[0].astype(F)
    for k in range(1, NC):
        w = w + wr[k].astype(F)
    w2[r] = w.astype(B)
    s2 = row_copies(lambda j: w2.at[r], w2.at[r], p2s, p2r)
    start(s2)
    wait(t2)
    t3 = col_copies(lambda j: tb.at[c], tb.at[c], t3s, t3r)
    start(t3)
    wait(s2)
    w = w2[0].astype(F)
    for k in range(1, NR):
        w = w + w2[k].astype(F)
    w3[share(c)] = w.astype(B)
    s3 = col_copies(lambda j: w3.at[share(c)], w3.at[share(c)], p3s, p3r)
    start(s3)

    scale = 1.0 / 1024
    wait(t3)
    tf = tb[...].astype(F)
    row_all = jnp.swapaxes(tf[:, :, :8], 0, 1).reshape(1024, 128).astype(B)
    col_all = tf[:, :, 8:].reshape(1024, 128).astype(B)
    cot_all = nt(row_all, prow[...]) + nt(col_all, pcol[...])
    cots[...] = cot_all
    cb = cot_all.astype(B)
    gsh = nt(cb, own_down[...])
    gsu = (gsh * si12[...]).astype(B)
    gsg = (gsh * slope12[...]).astype(B)
    osgate[...] = tn(gsg, nball[...])[:12] * scale
    osup[...] = tn(gsu, nball[...])[:12] * scale
    osdown[...] = tn(h12[...], cb)[:12] * scale
    opr[...] = tn(uall[...], row_all) * scale
    opc[...] = tn(uall[...], col_all) * scale
    c8 = cots[pl.ds(pl.multiple_of(joint * 8, 8), 8), :]
    g8 = nt(c8.astype(B), sdown[...])
    gu8 = (g8 * s_silu).astype(B)
    gg8 = (g8 * s_up * (s_sig + s_silu * (1.0 - s_sig))).astype(B)
    gn8 = nt(gg8, sgate[...]) + nt(gu8, sup[...])
    osg[...] = (
        c8 + inv_rms * (gn8 - normed * jnp.mean(gn8 * normed, axis=-1, keepdims=True))
    ).astype(B)

    wait(s3)
    for k in range(4):
        ks = slice(k * 128, (k + 1) * 128)
        oup[:, ks] = w3[k * 128:(k + 1) * 128].astype(F) * scale
        ogate[:, ks] = w3[512 + k * 128:640 + k * 128].astype(F) * scale
        odown[ks, :] = jnp.transpose(w3[1024 + k * 128:1152 + k * 128].astype(F)) * scale
    ohead[...] = w3[1536:1664].astype(F) * scale
    orel[...] = (w3[1664:1792].astype(F) * scale)[:65]

    sent_mirror(1)
    for b in range(4):
        i0 = (b % 2) * 64 + (b // 2) * 32
        pltpu.make_async_copy(ogv.at[pl.ds(i0, BR)], og.at[pl.ds(i0, BR)], out_sem.at[b]).wait()


def hand_over(*refs):
    ins, outs, held, sem_in, sem_out = refs[:12], refs[12:24], refs[24:36], refs[36], refs[37]
    parts = []
    for k in range(12):
        if k == 0:
            parts += [(k, pl.ds(p * 32, 32)) for p in range(4)]
        else:
            parts += [(k, slice(None))]
    into = [
        pltpu.make_async_copy(ins[k].at[rows], held[k].at[rows], sem_in.at[n])
        for n, (k, rows) in enumerate(parts)
    ]
    out = [
        pltpu.make_async_copy(held[k].at[rows], outs[k].at[rows], sem_out.at[n])
        for n, (k, rows) in enumerate(parts)
    ]
    for cp in into:
        cp.start()
    for a, b in zip(into, out):
        a.wait()
        b.start()
    for cp in out:
        cp.wait()


def local(
    pair_repr, logit_cotangent, pair_mask, single_repr, token_index, pair_up, pair_gate, pair_down,
    head_weight, rel_table, proj_row, proj_col, single_gate, single_up, single_down,
):
    S = lambda shape, dtype=F: jax.ShapeDtypeStruct(shape, dtype)
    V = pl.BlockSpec(memory_space=pltpu.VMEM)
    H = pl.BlockSpec(memory_space=pl.ANY)
    vm = lambda *shape: pltpu.VMEM(shape, F)
    vb = lambda *shape: pltpu.VMEM(shape, B)
    dma = lambda *shape: pltpu.SemaphoreType.DMA(shape)
    outs = pl.pallas_call(
        kernel,
        out_shape=(
            S((128, 64, 128), B), S((8, 384), B), S((128, 512)), S((128, 512)), S((512, 128)),
            S((128, 128)), S((65, 128)), S((384, 128)), S((384, 128)), S((12, 384)), S((12, 384)),
            S((12, 384)),
        ),
        in_specs=[H, H, V, V, V, pl.BlockSpec(memory_space=pltpu.SMEM)] + [V] * 7 + [H] * 3,
        out_specs=[H] + [V] * 11,
        scratch_shapes=[
            vb(128, 64, 128), vb(128, 64, 128), vb(128, 64, 128),
            pltpu.VMEM((64, 128), jnp.int32), pltpu.VMEM((64, 128), jnp.int32), vm(128, 128), vm(128, 128),
            vm(4, 64, 32), vm(2, 1024, 128), vb(2, 2, 16, 64, 128), vb(2, 2, 16, 64, 128),
            vb(8, 16, 2, 16, 128), vm(128, 128), vb(64, 128),
            vm(128, 128), vm(64, 128), vm(128, 1024), vm(128, 512), vm(128, 128), vm(128, 128),
            vb(1792, 128), vb(16, SHARE, 128), vb(8, SHARE, 128), vb(1792, 128),
            vm(16, 8, 128), vm(8, 8, 128), vb(16, 8, 16, 128), vm(1024, 384),
            vb(384, 1536), vb(384, 1536), vb(1536, 384), vb(16, 16, 128), vb(1024, 384), vb(1024, 384),
            vm(1024, 128), vm(1024, 128), vb(1024, 128), vb(128, 384),
            dma(5), dma(4), dma(2, 2), dma(2, 2), dma(16), dma(16), dma(8), dma(8), dma(8), dma(8), dma(8),
            dma(8), dma(16), dma(16),
            dma(16), dma(16), dma(16), dma(16), dma(8), dma(8), dma(8), dma(8), dma(8), dma(8),
            dma(16), dma(16), dma(16), dma(16),
        ],
        compiler_params=pltpu.CompilerParams(
            collective_id=0, has_side_effects=True, vmem_limit_bytes=60 << 20
        ),
        name="pair_backward",
    )(
        pair_repr, logit_cotangent, pair_mask.T, single_repr, token_index.reshape(8, 128), token_index,
        pair_up, pair_gate, pair_down, head_weight, rel_table, proj_row, proj_col,
        single_gate, single_up, single_down,
    )
    outs = pl.pallas_call(
        hand_over,
        out_shape=[S(o.shape, o.dtype) for o in outs],
        in_specs=[H] * 12,
        out_specs=[H] * 12,
        scratch_shapes=[pltpu.VMEM(o.shape, o.dtype) for o in outs] + [dma(15), dma(15)],
        name="hand_over",
    )(*outs)
    return (*outs[:9], outs[9].T, outs[10].T, outs[11])


def solution(mesh):
    strip = P(("row", "col"), None)
    return jax.shard_map(
        local,
        mesh=mesh,
        in_specs=(P("row", "col", None), P("row", "col", None), P("row", "col"), strip) + (P(),) * 11,
        out_specs=(P("row", "col", None), strip) + (P(),) * 7
        + (P(None, ("row", "col")), P(None, ("row", "col")), strip),
        check_vma=False,
    )
```
